1024 devices in a mesh: row: 16 (over z_lo, core), col: 64 (over z_hi, x, y).
Axes of the slice: x: 4, y: 4, z: 32 (z_hi: 4, z_lo: 8; z = z_hi * 8 + z_lo), core: 2. Of those that a mesh axis runs over, the one named last changes fastest.
Arguments:
- features: bfloat16 [32768, 512], P(('row', 'col')), may hold values from -6 to 6
- self_weight: bfloat16 [512, 512], replicated, may hold values from -0.25 to 0.25
- neigh_weight: bfloat16 [512, 512], replicated, may hold values from -0.25 to 0.25
- tiles: bfloat16 [16, 2048, 128, 128], P('row', 'col'), may hold values from 0 to 1, as said below
- tile_pos: int32 [16, 2048], P('row', 'col'), may hold values from 0 to 63, as said below
- tile_count: int32 [16, 64], P('row', 'col'), may hold values from 1 to 32, as said below
- degree: int32 [32768], P(('row', 'col')), may hold values from 256 to 2047
- cotangent: bfloat16 [32768, 512], P(('row', 'col')), may hold values from -0.029907227 to 0.029907227
Outputs:
- hidden: bfloat16 [32768, 512], P(('row', 'col'))
- self_weight_gradient: float32 [512, 512], replicated
- grad_neigh: float32 [512, 512], replicated
The draws below stay inside these ranges and needn't reach their ends.
Inputs may be any that keep to these rules, and one draw needn't show every extreme that they name: `tile_pos`: within each block's 32 slots the positions are distinct. `tile_count`: some block is full in every draw. `tiles`: entries are zero or between 0.25 and 1.
All inputs are finite; a program needn't handle non-finite values.
Results may differ from the reference program's by a relative error of at most 0.0055.
Values may be sent and summed in bfloat16 or wider, within the bound.
A program may use at most 32 MiB of HBM per device.

```python
import math
import jax
import jax.numpy as jnp
from jax import lax

WIDTH = 512
TILE = 128
NODE_DEV = 32
NODES = 32768
BLOCK_ROWS = 2048
TILE_ROWS = 16
TILE_COLS = 4
POSITIONS = 64
CAPACITY = 32
N_ROW = 16
N_COL = 64


def draw_tiles(key, part):
    key = jax.random.fold_in(key, 11)
    first_key, second_key = jax.random.split(key)
    shape = (N_ROW, N_COL * CAPACITY, TILE, TILE)
    chance = jax.random.uniform(first_key, shape, jnp.float32)
    magnitude = jnp.exp(jax.random.uniform(second_key, shape, jnp.float32, math.log(0.25), 0.0))
    tile_values_array = jnp.where(chance < 0.5, jnp.zeros_like(magnitude), magnitude)
    return tile_values_array.astype(jnp.bfloat16)


def first_slots(single_key):
    return jax.random.permutation(single_key, POSITIONS)[:CAPACITY].astype(jnp.int32)


def draw_tile_pos(key, part):
    key = jax.random.fold_in(key, 12)
    device_keys = jax.random.split(key, N_ROW * N_COL)
    chosen = jax.vmap(first_slots)(device_keys)
    return chosen.reshape(N_ROW, N_COL * CAPACITY)


def draw_tile_count(key, part):
    key = jax.random.fold_in(key, 13)
    first_key, second_key, third_key = jax.random.split(key, 3)
    left = jax.random.randint(first_key, (N_ROW * N_COL,), 0, CAPACITY + 1, jnp.int32)
    right = jax.random.randint(second_key, (N_ROW * N_COL,), 0, CAPACITY + 1, jnp.int32)
    counts = jnp.maximum(1, left * right // CAPACITY)
    fullest = jax.random.randint(third_key, (), 0, N_ROW * N_COL, jnp.int32)
    counts = jnp.where(jnp.arange(N_ROW * N_COL, dtype=jnp.int32) == fullest, CAPACITY, counts)
    return counts.reshape(N_ROW, N_COL).astype(jnp.int32)


def set_ends(drawn, key, low, top_value):
    place = [jax.random.randint(jax.random.fold_in(key, axis), (), 0, length) for axis, length in enumerate(drawn.shape)]
    main_axis = drawn.shape.index(max(drawn.shape))
    beside = place[:main_axis] + [(place[main_axis] + 1) % drawn.shape[main_axis]] + place[main_axis + 1:]
    return drawn.at[tuple(place)].set(low).at[tuple(beside)].set(top_value)


def levels(own_key, extent, shards, least, high):
    gain, own = 1.0, jax.random.fold_in(own_key, 6)
    for axis_at, blocks in shards:
        steps = jnp.exp(jax.random.uniform(jax.random.fold_in(own, axis_at), (blocks,), jnp.float32, least / len(shards), high / len(shards)))
        gain = gain * jnp.repeat(steps, extent[axis_at] // blocks).reshape([-1 if axis == axis_at else 1 for axis in range(len(extent))])
    return gain


def scatter_about(own_key, shape, width, limit, shards=(), kind=jnp.bfloat16):
    loudness = levels(own_key, shape, shards, -0.22, 0.18) if shards else 1.0
    result = jax.random.normal(own_key, shape, jnp.float32) * width * loudness
    return jnp.minimum(jnp.maximum(result, -limit), limit).astype(kind)


def setup_inputs(seed: int = 0) -> dict:
    keys = jax.random.split(jax.random.key(seed), 9)
    features = scatter_about(keys[0], (NODES, WIDTH), 1.0, 6.0, ((0, 1024),))
    self_weight = scatter_about(keys[1], (WIDTH, WIDTH), WIDTH ** -0.5, 0.25)
    neigh_weight = scatter_about(keys[2], (WIDTH, WIDTH), WIDTH ** -0.5, 0.25)
    tiles = draw_tiles(jax.random.fold_in(keys[8], 71), 0)
    tile_pos = draw_tile_pos(jax.random.fold_in(keys[8], 71), 0)
    tile_count = draw_tile_count(jax.random.fold_in(keys[8], 71), 0)
    degree = set_ends(jax.random.randint(keys[6], (NODES,), 256, 2048), jax.random.fold_in(keys[6], 1), 256, 2047).astype(jnp.int32)
    cotangent = scatter_about(keys[7], (NODES, WIDTH), 0.005, 0.029907227, ((0, 1024),))
    return dict(features=features, self_weight=self_weight, neigh_weight=neigh_weight, tiles=tiles, tile_pos=tile_pos, tile_count=tile_count, degree=degree, cotangent=cotangent)


def reference(features, self_weight, neigh_weight, tiles, tile_pos, tile_count, degree, cotangent):
    panels = features.reshape(N_ROW, N_COL, NODE_DEV, WIDTH)

    def device_block(counter, running):
        counter = jnp.asarray(counter).astype(jnp.int32)
        row_index = counter // N_COL
        col_index = counter % N_COL
        column_panel = lax.dynamic_index_in_dim(panels, col_index, 1, keepdims=False)
        by_tile = column_panel.reshape(TILE_COLS, TILE, WIDTH)
        tile_values_array = lax.dynamic_slice(tiles, (row_index, col_index * CAPACITY, jnp.int32(0), jnp.int32(0)), (1, CAPACITY, TILE, TILE))[0]
        positions = lax.dynamic_slice(tile_pos, (row_index, col_index * CAPACITY), (1, CAPACITY))[0]
        live_count = lax.dynamic_slice(tile_count, (row_index, col_index), (1, 1))[0, 0]
        live_slots = jnp.arange(CAPACITY, dtype=jnp.int32) < live_count
        input_features = by_tile[positions % TILE_COLS]
        partial_products = jnp.einsum('tew,twn->ten', tile_values_array.astype(jnp.float32), input_features.astype(jnp.float32))
        partial_products = jnp.where(live_slots[:, None, None], partial_products, jnp.zeros_like(partial_products))
        block = jnp.zeros((TILE_ROWS, TILE, WIDTH), partial_products.dtype).at[positions // TILE_COLS].add(partial_products)
        block = block.reshape(BLOCK_ROWS, WIDTH)
        starting = row_index * BLOCK_ROWS
        current = lax.dynamic_slice_in_dim(running, starting, BLOCK_ROWS, 0)
        return lax.dynamic_update_slice_in_dim(running, current + block, starting, 0)
    sums = lax.fori_loop(0, N_ROW * N_COL, device_block, jnp.zeros((NODES, WIDTH), jnp.float32))
    scale = lax.rsqrt(degree.astype(jnp.float32))
    aggregated = (sums * scale[:, None]).astype(jnp.bfloat16)
    before = jnp.dot(features, self_weight, preferred_element_type=jnp.float32) + jnp.dot(aggregated, neigh_weight, preferred_element_type=jnp.float32)
    sigma = jax.nn.sigmoid(before)
    hidden = (before * sigma).astype(jnp.bfloat16)
    gated = (cotangent.astype(jnp.float32) * sigma * (1.0 + before * (1.0 - sigma))).astype(jnp.bfloat16)
    self_weight_gradient = jnp.dot(features.T, gated, preferred_element_type=jnp.float32)
    grad_neigh = jnp.dot(aggregated.T, gated, preferred_element_type=jnp.float32)
    return (hidden, self_weight_gradient, grad_neigh)
```

```python
import jax
import jax.numpy as jnp
from jax import lax
from jax.experimental import pallas as pl
from jax.experimental.pallas import tpu as pltpu
from jax.sharding import PartitionSpec as P

MESH = pl.DeviceIdType.MESH
BF16, F32 = jnp.bfloat16, jnp.float32
WIDTH, TILE, ND = 512, 128, 32
HALF = WIDTH // 2


def flip(value, mask, bits):
    out = 0
    for k in range(bits):
        bit = lax.rem(lax.div(value, 1 << k), 2)
        out = out + (1 << k) * ((1 - bit) if (mask >> k) & 1 else bit)
    return out


def mix(value, other, bits):
    out = 0
    for k in range(bits):
        a = lax.rem(lax.div(value, 1 << k), 2)
        b = lax.rem(lax.div(other, 1 << k), 2)
        out = out + (1 << k) * (a + b - 2 * a * b)
    return out


def rows_at(index, count):
    return pl.ds(pl.multiple_of(index * count, count), count)


def kernel(
    features_ref, self_weight_ref, neigh_weight_ref, tiles_ref, slots_ref, degree_ref, cotangent_ref,
    hidden_ref, grads_ref,
    tiles_v, self_v, neigh_v, dense, panel, part0, part1, in_a0, in_a1, mid0, mid1, in_b0, in_b1,
    block, in_c, other, left, gated, left_in, gated_in, section, in_z, groups, final,
    load_sem, ag_s, ag_r, agc_s, agc_r, a_s, a_r, b_s, b_r, c_s, c_r, f_s, f_r, l_s, l_r, g_s, g_r,
    z_s, z_r, zs_s, zs_r, za_s, za_r, xy_s, xy_r, xc_s, xc_r,
):
    row, col = lax.axis_index("row"), lax.axis_index("col")
    core, z_lo = lax.rem(row, 2), lax.div(row, 2)
    z = lax.div(col, 16) * 8 + z_lo
    x, y = lax.rem(lax.div(col, 4), 4), lax.rem(col, 4)
    z_in, z_group = lax.rem(z, 4), lax.div(z, 4)

    def peer(dz=0, dx=0, dy=0, dc=0):
        zp, xp, yp, cp = flip(z, dz, 5), flip(x, dx, 2), flip(y, dy, 2), flip(core, dc, 1)
        return (lax.rem(zp, 8) * 2 + cp, lax.div(zp, 8) * 16 + xp * 4 + yp)

    def send(src, dst, ssem, rsem, to):
        copy = pltpu.make_async_remote_copy(
            src_ref=src, dst_ref=dst, send_sem=ssem, recv_sem=rsem, device_id=to, device_id_type=MESH
        )
        copy.start()
        sent.append(copy)
        return copy

    sent = []
    loads = [
        pltpu.make_async_copy(tiles_ref, tiles_v, load_sem.at[0]),
        pltpu.make_async_copy(self_weight_ref, self_v, load_sem.at[1]),
        pltpu.make_async_copy(neigh_weight_ref, neigh_v, load_sem.at[2]),
    ]
    for load in loads:
        load.start()

    partner = peer(dc=1)
    plane = [(m // 4, m % 4) for m in range(1, 16)]
    peers = [partner]
    peers += [peer(dz=m) for m in range(1, 8)]
    peers += [peer(dz=m) for m in (8, 12, 16, 20, 24, 28)]
    peers += [peer(dx=dx, dy=dy) for dx, dy in plane]
    barrier = pltpu.get_barrier_semaphore()
    for device in peers:
        pl.semaphore_signal(barrier, inc=1, device_id=device, device_id_type=MESH)

    panel[rows_at(row, ND), :] = features_ref[...]
    loads[0].wait()

    def place(t, carry):
        dz = mix(lax.div(t, 4), lax.div(col, 16), 2)
        dx = mix(lax.rem(t, 4), x, 2)
        for q in range(4):
            slot = slots_ref[t * 4 + q]
            tile = tiles_v[jnp.maximum(slot, 0)]
            tile = jnp.where(slot >= 0, tile, jnp.zeros_like(tile))
            for yc in range(4):
                dy = mix(jnp.int32(yc), y, 2)
                dense[dx * 4 + dy, rows_at(dz, ND), q * TILE : (q + 1) * TILE] = tile[yc * ND : (yc + 1) * ND]
        return carry

    lax.fori_loop(0, 16, place, 0)
    pl.semaphore_wait(barrier, len(peers))

    mine = rows_at(row, ND)
    gather = [
        send(features_ref, panel.at[mine, :], ag_s.at[m], ag_r.at[m], peer(dz=m)) for m in range(7, 0, -1)
    ][::-1]
    across = [send(features_ref, panel.at[mine, :], agc_s.at[0], agc_r.at[0], partner)]
    loads[1].wait()
    own_part = jnp.dot(features_ref[...], self_v[...], preferred_element_type=F32)
    for m in range(1, 8):
        gather[m - 1].wait_recv()
        theirs = panel.at[rows_at(flip(z_lo, m, 3) * 2 + core, ND), :]
        across.append(send(theirs, theirs, agc_s.at[m], agc_r.at[m], partner))
    for copy in across:
        copy.wait_recv()

    first, second = [], []
    for dx in (2, 1, 3, 0):
        for part in range(2):
            lhs = dense[dx * 4 + part * 2 : dx * 4 + part * 2 + 2].reshape(2 * TILE, WIDTH)
            product = jnp.dot(lhs, panel[...], preferred_element_type=F32).astype(BF16)
            for k in range(2):
                dy = part * 2 + k
                part0[dx, dy] = product[k * TILE : (k + 1) * TILE, :HALF]
                part1[dy, dx] = product[k * TILE : (k + 1) * TILE, HALF:]
        if dx:
            first.append(send(part0.at[dx], in_a0.at[dx], a_s.at[dx], a_r.at[dx], peer(dx=dx)))
    for dy in (2, 1, 3):
        second.append(send(part1.at[dy], in_a1.at[dy], a_s.at[4 + dy], a_r.at[4 + dy], peer(dy=dy)))

    def total(own, parts):
        out = own.astype(F32)
        for value in parts:
            out = out + value.astype(F32)
        return out

    for copy in first:
        copy.wait_recv()
    first = []
    for k in (2, 1, 3, 0):
        mid0[k] = total(part0[0, k], [in_a0[m, k] for m in (1, 2, 3)]).astype(BF16)
        if k:
            first.append(send(mid0.at[k], in_b0.at[k], b_s.at[k], b_r.at[k], peer(dy=k)))
    for copy in second:
        copy.wait_recv()
    second = []
    for k in (2, 1, 3, 0):
        mid1[k] = total(part1[0, k], [in_a1[m, k] for m in (1, 2, 3)]).astype(BF16)
        if k:
            second.append(send(mid1.at[k], in_b1.at[k], b_s.at[4 + k], b_r.at[4 + k], peer(dx=k)))
    for copy in first:
        copy.wait_recv()
    low = total(mid0[0], [in_b0[m] for m in (1, 2, 3)]).astype(BF16)
    for k in range(4):
        block[k, :, :HALF] = low[k * ND : (k + 1) * ND]
    for copy in second:
        copy.wait_recv()
    high = total(mid1[0], [in_b1[m] for m in (1, 2, 3)]).astype(BF16)
    for k in range(4):
        block[k, :, HALF:] = high[k * ND : (k + 1) * ND]
    far = [send(block.at[k], in_c.at[k], c_s.at[k], c_r.at[k], peer(dz=8 * k)) for k in (2, 1, 3)]
    loads[2].wait()
    degree = jnp.broadcast_to(degree_ref[...].astype(F32), (ND, ND))
    eye = lax.broadcasted_iota(jnp.int32, (ND, ND), 0) == lax.broadcasted_iota(jnp.int32, (ND, ND), 1)
    scale = lax.rsqrt(jnp.sum(jnp.where(eye, degree, 0.0), axis=1, keepdims=True))
    for copy in far:
        copy.wait_recv()
    sums = total(block[0], [in_c[k] for k in (1, 2, 3)])

    aggregated = (sums * scale).astype(BF16)
    before = own_part + jnp.dot(aggregated, neigh_v[...], preferred_element_type=F32)
    sigma = 1.0 / (1.0 + jnp.exp(-before))
    gate = (cotangent_ref[...].astype(F32) * sigma * (1.0 + before * (1.0 - sigma))).astype(BF16)
    hidden_ref[...] = (before * sigma).astype(BF16)
    other[0] = features_ref[...]
    other[1] = aggregated
    gated[0] = gate

    pair = [
        send(gated.at[0], gated.at[1], f_s.at[0], f_r.at[0], partner),
        send(other.at[1 - core], left.at[1], f_s.at[1], f_r.at[1], partner),
    ]
    left[0] = other[core]
    for copy in pair:
        copy.wait_recv()
    swaps = []
    for dx, dy in plane:
        m = dx * 4 + dy
        lanes_x = rows_at(flip(x, dx, 2), TILE)
        lanes_y = rows_at(flip(y, dy, 2), TILE)
        to = peer(dx=dx, dy=dy)
        swaps.append(send(left.at[:, :, lanes_x], left_in.at[m], l_s.at[m], l_r.at[m], to))
        swaps.append(send(gated.at[:, :, lanes_y], gated_in.at[m], g_s.at[m], g_r.at[m], to))
    left_in[0] = left[:, :, rows_at(x, TILE)]
    gated_in[0] = gated[:, :, rows_at(y, TILE)]
    for copy in swaps:
        copy.wait_recv()
    section[...] = lax.dot_general(
        left_in[...].reshape(16 * 2 * ND, TILE),
        gated_in[...].reshape(16 * 2 * ND, TILE),
        (((0,), (0,)), ((), ())),
        preferred_element_type=F32,
    ).reshape(4, ND, TILE)

    near = [
        send(section.at[flip(z_in, m, 2)], in_z.at[m], z_s.at[m], z_r.at[m], peer(dz=m)) for m in (2, 1, 3)
    ]
    for copy in near:
        copy.wait_recv()
    groups[z_group] = (section[z_in] + in_z[1] + in_z[2] + in_z[3]).astype(BF16)
    spread = [
        send(groups.at[z_group], groups.at[z_group], zs_s.at[m], zs_r.at[m], peer(dz=4 * m))
        for m in (4, 3, 5, 2, 6, 1, 7)
    ]
    for copy in spread:
        copy.wait_recv()
    final[rows_at(z_in, ND), :] = total(groups[0], [groups[k] for k in range(1, 8)]).astype(BF16)
    own_rows = final.at[rows_at(z_in, ND), :]
    back = [send(own_rows, own_rows, za_s.at[m], za_r.at[m], peer(dz=m)) for m in (2, 1, 3)]
    for copy in back:
        copy.wait_recv()

    here = grads_ref.at[core, x, :, rows_at(y, TILE)]
    out = [send(final, here, xy_s.at[dx * 4 + dy], xy_r.at[dx * 4 + dy], peer(dx=dx, dy=dy)) for dx, dy in plane]
    last = [send(final, here, xc_s.at[0], xc_r.at[0], partner)]
    grads_ref[core, x, :, rows_at(y, TILE)] = final[...]
    for (dx, dy), copy in zip(plane, out):
        copy.wait_recv()
        there = grads_ref.at[core, flip(x, dx, 2), :, rows_at(flip(y, dy, 2), TILE)]
        m = dx * 4 + dy
        last.append(send(there, there, xc_s.at[m], xc_r.at[m], partner))
    for copy in last:
        copy.wait_recv()
    for copy in sent:
        copy.wait_send()


def per_device(features, self_weight, neigh_weight, tiles, tile_pos, tile_count, degree, cotangent):
    capacity = tiles.shape[1]
    order = jnp.arange(capacity, dtype=jnp.int32)
    hit = (tile_pos[0][None, :] == jnp.arange(64, dtype=jnp.int32)[:, None]) & (order < tile_count[0, 0])[None, :]
    slots = jnp.max(jnp.where(hit, order[None, :], -1), axis=1)
    vmem, hbm = pl.BlockSpec(memory_space=pltpu.VMEM), pl.BlockSpec(memory_space=pl.ANY)
    dma = pltpu.SemaphoreType.DMA
    hidden, grads = pl.pallas_call(
        kernel,
        out_shape=(
            jax.ShapeDtypeStruct((ND, WIDTH), BF16),
            jax.ShapeDtypeStruct((2, 4, TILE, WIDTH), BF16),
        ),
        in_specs=[vmem, hbm, hbm, hbm, pl.BlockSpec(memory_space=pltpu.SMEM), vmem, vmem],
        out_specs=(vmem, vmem),
        scratch_shapes=[
            pltpu.VMEM((capacity, TILE, TILE), BF16),
            pltpu.VMEM((WIDTH, WIDTH), BF16),
            pltpu.VMEM((WIDTH, WIDTH), BF16),
            pltpu.VMEM((16, TILE, WIDTH), BF16),
            pltpu.VMEM((WIDTH, WIDTH), BF16),
            pltpu.VMEM((4, 4, TILE, HALF), BF16),
            pltpu.VMEM((4, 4, TILE, HALF), BF16),
            pltpu.VMEM((4, 4, TILE, HALF), BF16),
            pltpu.VMEM((4, 4, TILE, HALF), BF16),
            pltpu.VMEM((4, TILE, HALF), BF16),
            pltpu.VMEM((4, TILE, HALF), BF16),
            pltpu.VMEM((4, TILE, HALF), BF16),
            pltpu.VMEM((4, TILE, HALF), BF16),
            pltpu.VMEM((4, ND, WIDTH), BF16),
            pltpu.VMEM((4, ND, WIDTH), BF16),
            pltpu.VMEM((2, ND, WIDTH), BF16),
            pltpu.VMEM((2, ND, WIDTH), BF16),
            pltpu.VMEM((2, ND, WIDTH), BF16),
            pltpu.VMEM((16, 2, ND, TILE), BF16),
            pltpu.VMEM((16, 2, ND, TILE), BF16),
            pltpu.VMEM((4, ND, TILE), F32),
            pltpu.VMEM((4, ND, TILE), F32),
            pltpu.VMEM((8, ND, TILE), BF16),
            pltpu.VMEM((TILE, TILE), BF16),
            dma((3,)),
            *[dma((8,))] * 8,
            *[dma((4,))] * 2,
            *[dma((2,))] * 2,
            *[dma((16,))] * 4,
            *[dma((4,))] * 2,
            *[dma((8,))] * 2,
            *[dma((4,))] * 2,
            *[dma((16,))] * 4,
        ],
        compiler_params=pltpu.CompilerParams(
            collective_id=0, has_side_effects=True, vmem_limit_bytes=40 * 1024 * 1024
        ),
        name="sage_layer",
    )(features, self_weight, neigh_weight, tiles[0], slots, degree[None, :], cotangent)
    grads = grads.reshape(2, WIDTH, WIDTH)
    return (hidden, grads[0].astype(F32), grads[1].astype(F32))


def solution(mesh):
    in_specs = (
        P(("row", "col"), None),
        P(),
        P(),
        P("row", "col", None, None),
        P("row", "col"),
        P("row", "col"),
        P(("row", "col")),
        P(("row", "col"), None),
    )
    out_specs = (P(("row", "col"), None), P(), P())
    return jax.shard_map(
        per_device, mesh=mesh, in_specs=in_specs, out_specs=out_specs, check_vma=False
    )
```

```python
import jax
import jax.numpy as jnp
from jax import lax
from jax.experimental import pallas as pl
from jax.experimental.pallas import tpu as pltpu
from jax.sharding import PartitionSpec as P

MESH = pl.DeviceIdType.MESH
BF16, F32 = jnp.bfloat16, jnp.float32
WIDTH, TILE, ND = 512, 128, 32
HALF = WIDTH // 2


def flip(value, mask, bits):
    out = 0
    for k in range(bits):
        bit = lax.rem(lax.div(value, 1 << k), 2)
        out = out + (1 << k) * ((1 - bit) if (mask >> k) & 1 else bit)
    return out


def mix(value, other, bits):
    out = 0
    for k in range(bits):
        a = lax.rem(lax.div(value, 1 << k), 2)
        b = lax.rem(lax.div(other, 1 << k), 2)
        out = out + (1 << k) * (a + b - 2 * a * b)
    return out


def rows_at(index, count):
    return pl.ds(pl.multiple_of(index * count, count), count)


def kernel(
    features_hbm, self_weight_ref, neigh_weight_ref, tiles_ref, slots_hbm, degree_hbm, cotangent_hbm,
    hidden_ref, grads_ref,
    features_ref, slots_ref, degree_ref, cotangent_ref, tiles_v, self_v, neigh_v, dense, panel, part0, part1, own0, own1, in_a0, in_a1, mid0, mid1, in_b0, in_b1,
    block, own_sums, in_c, left_over, left, gated, left_in, gated_in, section, in_z, groups, final, parts,
    word, load_sem, ag_s, ag_r, agc_s, agc_r, a_s, a_r, b_s, b_r, c_s, c_r, f_s, f_r, l_s, l_r, g_s, g_r,
    z_s, z_r, zs_s, zs_r, za_s, za_r, xy_s, xy_r, xc_s, xc_r,
):
    row, col = lax.axis_index("row"), lax.axis_index("col")
    core, z_lo = lax.rem(row, 2), lax.div(row, 2)
    z = lax.div(col, 16) * 8 + z_lo
    x, y = lax.rem(lax.div(col, 4), 4), lax.rem(col, 4)
    z_in, z_group = lax.rem(z, 4), lax.div(z, 4)

    def peer(dz=0, dx=0, dy=0, dc=0):
        zp, xp, yp, cp = flip(z, dz, 5), flip(x, dx, 2), flip(y, dy, 2), flip(core, dc, 1)
        return (lax.rem(zp, 8) * 2 + cp, lax.div(zp, 8) * 16 + xp * 4 + yp)

    def send(src, dst, ssem, rsem, to):
        copy = pltpu.make_async_remote_copy(
            src_ref=src, dst_ref=dst, send_sem=ssem, recv_sem=rsem, device_id=to, device_id_type=MESH
        )
        copy.start()
        sent.append(copy)
        return copy

    sent = []
    sources = (features_hbm, slots_hbm, tiles_ref, self_weight_ref, neigh_weight_ref, degree_hbm, cotangent_hbm)
    targets = (features_ref, slots_ref, tiles_v, self_v, neigh_v, degree_ref, cotangent_ref)
    loads = [
        pltpu.make_async_copy(source, target, load_sem.at[k])
        for k, (source, target) in enumerate(zip(sources, targets))
    ]
    for load in loads:
        load.start()

    partner = peer(dc=1)
    plane = [(m // 4, m % 4) for m in range(1, 16)]
    peers = [partner]
    peers += [peer(dz=m) for m in range(1, 8)]
    peers += [peer(dz=m) for m in (8, 24)]
    peers += [peer(dx=dx, dy=dy) for dx, dy in plane]
    barrier = pltpu.get_barrier_semaphore()
    for device in peers:
        pl.semaphore_signal(barrier, inc=1, device_id=device, device_id_type=MESH)

    loads[0].wait()
    for h in range(2):
        panel[h, rows_at(row, ND), :] = features_ref[:, h * HALF : (h + 1) * HALF]

    pl.semaphore_wait(barrier, len(peers))
    for m in (4, 8, 24):
        pl.semaphore_signal(word.at[0], inc=1, device_id=peer(dz=m), device_id_type=MESH)

    mine = rows_at(row, ND)
    halves = [features_ref.at[:, h * HALF : (h + 1) * HALF] for h in range(2)]
    gather = [
        {
            m: send(halves[h], panel.at[h, mine, :], ag_s.at[h, m], ag_r.at[h, m], peer(dz=m)) for m in (4, 2, 1)
        }
        for h in range(2)
    ]
    across = [
        [send(halves[h], panel.at[h, mine, :], agc_s.at[h, 0], agc_r.at[h, 0], partner)] for h in range(2)
    ]

    for load in loads[1:3]:
        load.wait()

    def place(t, carry):
        dz = mix(lax.div(t, 4), lax.div(col, 16), 2)
        dx = mix(lax.rem(t, 4), x, 2)
        for q in range(4):
            slot = slots_ref[t * 4 + q]
            tile = tiles_v[jnp.maximum(slot, 0)]
            tile = jnp.where(slot >= 0, tile, jnp.zeros_like(tile))
            for yc in range(4):
                dy = mix(jnp.int32(yc), y, 2)
                dense[dx * 4 + dy, rows_at(dz, ND), q * TILE : (q + 1) * TILE] = tile[yc * ND : (yc + 1) * ND]
        return carry

    lax.fori_loop(0, 16, place, 0)

    def arrived(h, m, passed_on):
        gather[h][m].wait_recv()
        theirs = panel.at[h, rows_at(flip(z_lo, m, 3) * 2 + core, ND), :]
        for step in passed_on:
            origin = m + step
            gather[h][origin] = send(theirs, theirs, ag_s.at[h, origin], ag_r.at[h, origin], peer(dz=step))
        across[h].append(send(theirs, theirs, agc_s.at[h, m], agc_r.at[h, m], partner))

    for h in range(2):
        arrived(h, 4, (2, 1))
        arrived(h, 2, (1,))
        arrived(h, 6, (1,))
    loads[3].wait()

    along_x, along_y = [], []
    for h in range(2):
        for m in (1, 3, 5, 7):
            arrived(h, m, ())
        for copy in across[h]:
            copy.wait_recv()
        first, second = {}, {}
        for dx in (2, 1, 3, 0):
            lhs = dense[dx * 4 : dx * 4 + 4].reshape(4 * TILE, WIDTH)
            product = jnp.dot(lhs, panel[h], preferred_element_type=F32)
            for dy in range(4):
                rows = product[dy * TILE : (dy + 1) * TILE]
                if dx:
                    part0[h, dx, dy] = rows[:, :TILE].astype(BF16)
                else:
                    own0[h, dy] = rows[:, :TILE]
                if dy:
                    part1[h, dy, dx] = rows[:, TILE:].astype(BF16)
                else:
                    own1[h, dx] = rows[:, TILE:]
            if dx:
                first[dx] = send(part0.at[h, dx], in_a0.at[h, dx], a_s.at[h, dx], a_r.at[h, dx], peer(dx=dx))
        for dy in (2, 1, 3):
            second[dy] = send(part1.at[h, dy], in_a1.at[h, dy], a_s.at[h, 4 + dy], a_r.at[h, 4 + dy], peer(dy=dy))
        along_x.append(first)
        along_y.append(second)

    def total(own, parts):
        out = own.astype(F32)
        for value in parts:
            out = out + value.astype(F32)
        return out

    far = []
    for h in range(2):
        first, second = {}, {}
        for copy in along_x[h].values():
            copy.wait_recv()
        for k in (2, 1, 3, 0):
            value = total(own0[h, k], [in_a0[h, m, k] for m in (1, 2, 3)])
            if k:
                mid0[h, k] = value.astype(BF16)
                first[k] = send(mid0.at[h, k], in_b0.at[h, k], b_s.at[h, k], b_r.at[h, k], peer(dy=k))
            else:
                own0[h, 0] = value
        for copy in along_y[h].values():
            copy.wait_recv()
        for k in (2, 1, 3, 0):
            value = total(own1[h, k], [in_a1[h, m, k] for m in (1, 2, 3)])
            if k:
                mid1[h, k] = value.astype(BF16)
                second[k] = send(mid1.at[h, k], in_b1.at[h, k], b_s.at[h, 4 + k], b_r.at[h, 4 + k], peer(dx=k))
            else:
                own1[h, 0] = value
        for copy in first.values():
            copy.wait_recv()
        if h == 0:
            pl.semaphore_wait(word.at[0], 3)
            pl.semaphore_signal(word.at[1], inc=1, device_id=peer(dz=4), device_id_type=MESH)
        low = total(own0[h, 0], [in_b0[h, m] for m in (1, 2, 3)])
        for copy in second.values():
            copy.wait_recv()
        high = total(own1[h, 0], [in_b1[h, m] for m in (1, 2, 3)])
        for k in (2, 1, 3):
            block[h, k, :, :TILE] = low[k * ND : (k + 1) * ND].astype(BF16)
            block[h, k, :, TILE:] = high[k * ND : (k + 1) * ND].astype(BF16)
            far.append(send(block.at[h, k], in_c.at[h, k], c_s.at[h, k], c_r.at[h, k], peer(dz=8 * k)))
        own_sums[:, h * HALF : h * HALF + TILE] = low[:ND]
        own_sums[:, h * HALF + TILE : (h + 1) * HALF] = high[:ND]

    def spread_left():
        for dx, dy in plane:
            m = dx * 4 + dy
            lanes = rows_at(flip(x, dx, 2), TILE)
            left_copy(m, lanes, peer(dx=dx, dy=dy)).start()
        left_in[0] = left[:, :, rows_at(x, TILE)]

    def left_copy(m, lanes, to):
        return pltpu.make_async_remote_copy(
            src_ref=left.at[:, :, lanes], dst_ref=left_in.at[m], send_sem=l_s.at[m], recv_sem=l_r.at[m],
            device_id=to, device_id_type=MESH,
        )

    @pl.when(core == 0)
    def _():
        left[0] = features_ref[...]
        for h in range(2):
            left[1, :, h * HALF : (h + 1) * HALF] = panel[h, rows_at(row + 1, ND), :]
        spread_left()

    own_part = jnp.dot(features_ref[...], self_v[...], preferred_element_type=F32)
    for load in loads[4:]:
        load.wait()
    degree = jnp.broadcast_to(degree_ref[...].astype(F32), (ND, ND))
    eye = lax.broadcasted_iota(jnp.int32, (ND, ND), 0) == lax.broadcasted_iota(jnp.int32, (ND, ND), 1)
    scale = lax.rsqrt(jnp.sum(jnp.where(eye, degree, 0.0), axis=1, keepdims=True))
    for copy in far:
        copy.wait_recv()
    for h in range(2):
        lanes = slice(h * HALF, (h + 1) * HALF)
        own_sums[:, lanes] = total(own_sums[:, lanes], [in_c[h, k] for k in (1, 2, 3)])
    sums = own_sums[...]

    aggregated = (sums * scale).astype(BF16)
    before = own_part + jnp.dot(aggregated, neigh_v[...], preferred_element_type=F32)
    sigma = 1.0 / (1.0 + jnp.exp(-before))
    gate = (cotangent_ref[...].astype(F32) * sigma * (1.0 + before * (1.0 - sigma))).astype(BF16)
    hidden_ref[...] = (before * sigma).astype(BF16)
    gated[0] = gate
    pair = send(gated.at[0], gated.at[1], f_s.at[0], f_r.at[0], partner)
    hand_over = pltpu.make_async_remote_copy(
        src_ref=left_over, dst_ref=left.at[1], send_sem=f_s.at[1], recv_sem=f_r.at[1],
        device_id=partner, device_id_type=MESH,
    )

    @pl.when(core == 0)
    def _():
        left_over[...] = aggregated
        hand_over.start()

    @pl.when(core == 1)
    def _():
        left[0] = aggregated

    pair.wait_recv()
    swaps = []
    for dx, dy in plane:
        m = dx * 4 + dy
        lanes_y = rows_at(flip(y, dy, 2), TILE)
        swaps.append(send(gated.at[:, :, lanes_y], gated_in.at[m], g_s.at[m], g_r.at[m], peer(dx=dx, dy=dy)))

    @pl.when(core == 1)
    def _():
        hand_over.wait_recv()
        spread_left()

    gated_in[0] = gated[:, :, rows_at(y, TILE)]
    for copy in swaps:
        copy.wait_recv()
    lefts = [left_copy(dx * 4 + dy, rows_at(x, TILE), peer(dx=dx, dy=dy)) for dx, dy in plane]
    for copy in lefts:
        copy.wait_recv()
    section[...] = lax.dot_general(
        left_in[...].reshape(16 * 2 * ND, TILE),
        gated_in[...].reshape(16 * 2 * ND, TILE),
        (((0,), (0,)), ((), ())),
        preferred_element_type=F32,
    ).reshape(4, ND, TILE)

    near = [
        send(section.at[flip(z_in, m, 2)], in_z.at[m], z_s.at[m], z_r.at[m], peer(dz=m)) for m in (2, 1, 3)
    ]
    for copy in near:
        copy.wait_recv()
    groups[z_group] = (section[z_in] + in_z[1] + in_z[2] + in_z[3]).astype(BF16)
    pl.semaphore_wait(word.at[1], 1)
    spread = [
        send(groups.at[z_group], groups.at[z_group], zs_s.at[m], zs_r.at[m], peer(dz=4 * m))
        for m in (4, 3, 5, 2, 6, 1, 7)
    ]
    for copy in spread:
        copy.wait_recv()
    final[0] = total(groups[0], [groups[k] for k in range(1, 8)]).astype(BF16)
    back = [send(final.at[0], final.at[m], za_s.at[m], za_r.at[m], peer(dz=m)) for m in (2, 1, 3)]

    to_plane = [peer(dx=dx, dy=dy) for dx, dy in plane]
    out = [
        send(final.at[0], parts.at[core, x, y, 0], xy_s.at[0, m], xy_r.at[0, m], to)
        for m, to in enumerate(to_plane)
    ]
    for copy in back:
        copy.wait_recv()
    rest = parts.at[core, x, y, 1:4]
    more = [send(final.at[1:4], rest, xy_s.at[1, m], xy_r.at[1, m], to) for m, to in enumerate(to_plane)]
    last = [send(final, parts.at[core, x, y], xc_s.at[0], xc_r.at[0], partner)]

    def put(c, xb, yb, pieces):
        for m in range(4):
            grads_ref[rows_at(c * 16 + xb * 4 + flip(z_in, m, 2), ND), rows_at(yb, TILE)] = pieces[m]

    put(core, x, y, final[...])
    for m, (dx, dy) in enumerate(plane):
        out[m].wait_recv()
        more[m].wait_recv()
        xb, yb = flip(x, dx, 2), flip(y, dy, 2)
        theirs = parts.at[core, xb, yb]
        last.append(send(theirs, theirs, xc_s.at[dx * 4 + dy], xc_r.at[dx * 4 + dy], partner))
        put(core, xb, yb, parts[core, xb, yb])
    for (dx, dy), copy in zip([(0, 0)] + plane, last):
        copy.wait_recv()
        xb, yb = flip(x, dx, 2), flip(y, dy, 2)
        put(1 - core, xb, yb, parts[1 - core, xb, yb])
    for copy in lefts:
        copy.wait_send()

    @pl.when(core == 0)
    def _():
        hand_over.wait_send()

    for copy in sent:
        copy.wait_send()


def per_device(features, self_weight, neigh_weight, tiles, tile_pos, tile_count, degree, cotangent):
    capacity = tiles.shape[1]
    order = jnp.arange(capacity, dtype=jnp.int32)
    hit = (tile_pos[0][None, :] == jnp.arange(64, dtype=jnp.int32)[:, None]) & (order < tile_count[0, 0])[None, :]
    slots = jnp.max(jnp.where(hit, order[None, :], -1), axis=1)
    vmem, hbm = pl.BlockSpec(memory_space=pltpu.VMEM), pl.BlockSpec(memory_space=pltpu.HBM)
    dma = pltpu.SemaphoreType.DMA
    hidden, grads = pl.pallas_call(
        kernel,
        out_shape=(
            jax.ShapeDtypeStruct((ND, WIDTH), BF16),
            jax.ShapeDtypeStruct((2 * WIDTH, WIDTH), BF16),
        ),
        in_specs=[hbm] * 7,
        out_specs=(vmem, vmem),
        scratch_shapes=[
            pltpu.VMEM((ND, WIDTH), BF16),
            pltpu.SMEM((64,), jnp.int32),
            pltpu.VMEM((1, ND), jnp.int32),
            pltpu.VMEM((ND, WIDTH), BF16),
            pltpu.VMEM((capacity, TILE, TILE), BF16),
            pltpu.VMEM((WIDTH, WIDTH), BF16),
            pltpu.VMEM((WIDTH, WIDTH), BF16),
            pltpu.VMEM((16, TILE, WIDTH), BF16),
            pltpu.VMEM((2, WIDTH, HALF), BF16),
            pltpu.VMEM((2, 4, 4, TILE, TILE), BF16),
            pltpu.VMEM((2, 4, 4, TILE, TILE), BF16),
            pltpu.VMEM((2, 4, TILE, TILE), F32),
            pltpu.VMEM((2, 4, TILE, TILE), F32),
            pltpu.VMEM((2, 4, 4, TILE, TILE), BF16),
            pltpu.VMEM((2, 4, 4, TILE, TILE), BF16),
            pltpu.VMEM((2, 4, TILE, TILE), BF16),
            pltpu.VMEM((2, 4, TILE, TILE), BF16),
            pltpu.VMEM((2, 4, TILE, TILE), BF16),
            pltpu.VMEM((2, 4, TILE, TILE), BF16),
            pltpu.VMEM((2, 4, ND, HALF), BF16),
            pltpu.VMEM((ND, WIDTH), F32),
            pltpu.VMEM((2, 4, ND, HALF), BF16),
            pltpu.VMEM((ND, WIDTH), BF16),
            pltpu.VMEM((2, ND, WIDTH), BF16),
            pltpu.VMEM((2, ND, WIDTH), BF16),
            pltpu.VMEM((16, 2, ND, TILE), BF16),
            pltpu.VMEM((16, 2, ND, TILE), BF16),
            pltpu.VMEM((4, ND, TILE), F32),
            pltpu.VMEM((4, ND, TILE), F32),
            pltpu.VMEM((8, ND, TILE), BF16),
            pltpu.VMEM((4, ND, TILE), BF16),
            pltpu.VMEM((2, 4, 4, 4, ND, TILE), BF16),
            pltpu.SemaphoreType.REGULAR((2,)),
            dma((7,)),
            *[dma((2, 8))] * 8,
            *[dma((2, 4))] * 2,
            *[dma((2,))] * 2,
            *[dma((16,))] * 4,
            *[dma((4,))] * 2,
            *[dma((8,))] * 2,
            *[dma((4,))] * 2,
            *[dma((2, 16))] * 2,
            *[dma((16,))] * 2,
        ],
        compiler_params=pltpu.CompilerParams(
            collective_id=0, has_side_effects=True, vmem_limit_bytes=60 * 1024 * 1024
        ),
        name="sage_layer",
    )(features, self_weight, neigh_weight, tiles[0], slots, degree[None, :], cotangent)
    return (hidden, grads[:WIDTH].astype(F32), grads[WIDTH:].astype(F32))


def solution(mesh):
    in_specs = (
        P(("row", "col"), None),
        P(),
        P(),
        P("row", "col", None, None),
        P("row", "col"),
        P("row", "col"),
        P(("row", "col")),
        P(("row", "col"), None),
    )
    out_specs = (P(("row", "col"), None), P(), P())
    return jax.shard_map(
        per_device, mesh=mesh, in_specs=in_specs, out_specs=out_specs, check_vma=False
    )
```

```python
import jax
import jax.numpy as jnp
from jax import lax
from jax.experimental import pallas as pl
from jax.experimental.pallas import tpu as pltpu
from jax.sharding import PartitionSpec as P

MESH = pl.DeviceIdType.MESH
BF16, F32 = jnp.bfloat16, jnp.float32
WIDTH, TILE, ND = 512, 128, 32
HALF = WIDTH // 2


def flip(value, mask, bits):
    out = 0
    for k in range(bits):
        bit = lax.rem(lax.div(value, 1 << k), 2)
        out = out + (1 << k) * ((1 - bit) if (mask >> k) & 1 else bit)
    return out


def mix(value, other, bits):
    out = 0
    for k in range(bits):
        a = lax.rem(lax.div(value, 1 << k), 2)
        b = lax.rem(lax.div(other, 1 << k), 2)
        out = out + (1 << k) * (a + b - 2 * a * b)
    return out


def rows_at(index, count):
    return pl.ds(pl.multiple_of(index * count, count), count)


def kernel(
    features_hbm, self_weight_ref, neigh_weight_ref, tiles_ref, position_hbm, count_hbm, degree_hbm, cotangent_hbm,
    hidden_ref, grads_ref,
    features_ref, position_ref, count_ref, slots_v, slots_ref, degree_ref, cotangent_ref, tiles_v, self_v, neigh_v, dense, panel, part0, part1, own0, own1, in_a0, in_a1, mid0, mid1, in_b0, in_b1,
    block, own_sums, in_c, ours, left, gated, left_in, gated_in, section, in_z, groups, final, parts,
    word, load_sem, ag_s, ag_r, agc_s, agc_r, a_s, a_r, b_s, b_r, c_s, c_r, e_s, e_r, l_s, l_r, g_s, g_r,
    z_s, z_r, zs_s, zs_r, za_s, za_r, xy_s, xy_r, xc_s, xc_r,
):
    row, col = lax.axis_index("row"), lax.axis_index("col")
    core, z_lo = lax.rem(row, 2), lax.div(row, 2)
    z = lax.div(col, 16) * 8 + z_lo
    x, y = lax.rem(lax.div(col, 4), 4), lax.rem(col, 4)
    z_in, z_group = lax.rem(z, 4), lax.div(z, 4)

    def peer(dz=0, dx=0, dy=0, dc=0):
        zp, xp, yp, cp = flip(z, dz, 5), flip(x, dx, 2), flip(y, dy, 2), flip(core, dc, 1)
        return (lax.rem(zp, 8) * 2 + cp, lax.div(zp, 8) * 16 + xp * 4 + yp)

    def send(src, dst, ssem, rsem, to):
        copy = pltpu.make_async_remote_copy(
            src_ref=src, dst_ref=dst, send_sem=ssem, recv_sem=rsem, device_id=to, device_id_type=MESH
        )
        copy.start()
        sent.append(copy)
        return copy

    sent = []
    sources = (features_hbm, position_hbm, count_hbm, tiles_ref, self_weight_ref, neigh_weight_ref, degree_hbm, cotangent_hbm)
    targets = (features_ref, position_ref, count_ref, tiles_v, self_v, neigh_v, degree_ref, cotangent_ref)
    loads = [
        pltpu.make_async_copy(source, target, load_sem.at[k])
        for k, (source, target) in enumerate(zip(sources, targets))
    ]
    for load in loads:
        load.start()

    partner = peer(dc=1)
    plane = [(m // 4, m % 4) for m in range(1, 16)]
    peers = [partner]
    peers += [peer(dz=m) for m in range(1, 8)]
    peers += [peer(dz=m) for m in (8, 24)]
    peers += [peer(dx=dx, dy=dy, dc=dc) for dx, dy in plane for dc in range(2)]
    barrier = pltpu.get_barrier_semaphore()
    for device in peers:
        pl.semaphore_signal(barrier, inc=1, device_id=device, device_id_type=MESH)

    loads[0].wait()
    for h in range(2):
        panel[h, rows_at(row, ND), :] = features_ref[:, h * HALF : (h + 1) * HALF]

    pl.semaphore_wait(barrier, len(peers))
    for m in (4, 8, 24):
        pl.semaphore_signal(word.at[0], inc=1, device_id=peer(dz=m), device_id_type=MESH)

    mine = rows_at(row, ND)
    halves = [features_ref.at[:, h * HALF : (h + 1) * HALF] for h in range(2)]
    gather = [
        {
            m: send(halves[h], panel.at[h, mine, :], ag_s.at[h, m], ag_r.at[h, m], peer(dz=m)) for m in (4, 3, 2, 1)
        }
        for h in range(2)
    ]
    across = [
        [send(halves[h], panel.at[h, mine, :], agc_s.at[h, 0], agc_r.at[h, 0], partner)] for h in range(2)
    ]

    for load in loads[1:4]:
        load.wait()
    at = lax.broadcasted_iota(jnp.int32, (64, 32), 0)
    order = lax.broadcasted_iota(jnp.int32, (64, 32), 1)
    hit = jnp.broadcast_to(position_ref[...], (64, 32)) == at
    live = order < count_ref[0, 0]
    found = jnp.sum(jnp.where(hit & live, order + 1, 0), axis=1, keepdims=True) - 1
    slots_v[...] = jnp.broadcast_to(found, (64, TILE))
    to_scalars = pltpu.make_async_copy(slots_v, slots_ref, load_sem.at[8])
    to_scalars.start()
    to_scalars.wait()

    def place(t, carry):
        dz = mix(lax.div(t, 4), lax.div(col, 16), 2)
        dx = mix(lax.rem(t, 4), x, 2)
        for q in range(4):
            slot = slots_ref[t * 4 + q, 0]
            tile = tiles_v[jnp.maximum(slot, 0)]
            tile = jnp.where(slot >= 0, tile, jnp.zeros_like(tile))
            for yc in range(4):
                dy = mix(jnp.int32(yc), y, 2)
                dense[dx * 4 + dy, rows_at(dz, ND), q * TILE : (q + 1) * TILE] = tile[yc * ND : (yc + 1) * ND]
        return carry

    lax.fori_loop(0, 16, place, 0)

    def arrived(h, m, passed_on):
        gather[h][m].wait_recv()
        theirs = panel.at[h, rows_at(flip(z_lo, m, 3) * 2 + core, ND), :]
        for step in passed_on:
            origin = m + step
            gather[h][origin] = send(theirs, theirs, ag_s.at[h, origin], ag_r.at[h, origin], peer(dz=step))
        across[h].append(send(theirs, theirs, agc_s.at[h, m], agc_r.at[h, m], partner))

    for h in range(2):
        arrived(h, 4, (3, 2, 1))
    loads[4].wait()

    along_x, along_y = [], []
    for h in range(2):
        for m in (1, 2, 3, 5, 6, 7):
            arrived(h, m, ())
        for copy in across[h]:
            copy.wait_recv()
        first, second = {}, {}
        for dx in (2, 1, 3, 0):
            lhs = dense[dx * 4 : dx * 4 + 4].reshape(4 * TILE, WIDTH)
            product = jnp.dot(lhs, panel[h], preferred_element_type=F32)
            for dy in range(4):
                rows = product[dy * TILE : (dy + 1) * TILE]
                if dx:
                    part0[h, dx, dy] = rows[:, :TILE].astype(BF16)
                else:
                    own0[h, dy] = rows[:, :TILE]
                if dy:
                    part1[h, dy, dx] = rows[:, TILE:].astype(BF16)
                else:
                    own1[h, dx] = rows[:, TILE:]
            if dx:
                first[dx] = send(part0.at[h, dx], in_a0.at[h, dx], a_s.at[h, dx], a_r.at[h, dx], peer(dx=dx))
        for dy in (2, 1, 3):
            second[dy] = send(part1.at[h, dy], in_a1.at[h, dy], a_s.at[h, 4 + dy], a_r.at[h, 4 + dy], peer(dy=dy))
        along_x.append(first)
        along_y.append(second)

    def total(own, parts):
        out = own.astype(F32)
        for value in parts:
            out = out + value.astype(F32)
        return out

    far = []
    for h in range(2):
        first, second = {}, {}
        for copy in along_x[h].values():
            copy.wait_recv()
        for k in (2, 1, 3, 0):
            value = total(own0[h, k], [in_a0[h, m, k] for m in (1, 2, 3)])
            if k:
                mid0[h, k] = value.astype(BF16)
                first[k] = send(mid0.at[h, k], in_b0.at[h, k], b_s.at[h, k], b_r.at[h, k], peer(dy=k))
            else:
                own0[h, 0] = value
        for copy in along_y[h].values():
            copy.wait_recv()
        for k in (2, 1, 3, 0):
            value = total(own1[h, k], [in_a1[h, m, k] for m in (1, 2, 3)])
            if k:
                mid1[h, k] = value.astype(BF16)
                second[k] = send(mid1.at[h, k], in_b1.at[h, k], b_s.at[h, 4 + k], b_r.at[h, 4 + k], peer(dx=k))
            else:
                own1[h, 0] = value
        for copy in first.values():
            copy.wait_recv()
        if h == 0:
            pl.semaphore_wait(word.at[0], 3)
            pl.semaphore_signal(word.at[1], inc=1, device_id=peer(dz=4), device_id_type=MESH)
        low = total(own0[h, 0], [in_b0[h, m] for m in (1, 2, 3)])
        for copy in second.values():
            copy.wait_recv()
        high = total(own1[h, 0], [in_b1[h, m] for m in (1, 2, 3)])
        for k in (2, 1, 3):
            block[h, k, :, :TILE] = low[k * ND : (k + 1) * ND].astype(BF16)
            block[h, k, :, TILE:] = high[k * ND : (k + 1) * ND].astype(BF16)
            far.append(send(block.at[h, k], in_c.at[h, k], c_s.at[h, k], c_r.at[h, k], peer(dz=8 * k)))
        own_sums[:, h * HALF : h * HALF + TILE] = low[:ND]
        own_sums[:, h * HALF + TILE : (h + 1) * HALF] = high[:ND]

    def early_copy(m, dx, dy):
        return pltpu.make_async_remote_copy(
            src_ref=left.at[:, :, rows_at(flip(x, dx, 2), TILE)], dst_ref=left_in.at[m],
            send_sem=e_s.at[m], recv_sem=e_r.at[m], device_id=peer(dx=dx, dy=dy), device_id_type=MESH,
        )

    @pl.when(core == 0)
    def _():
        left[0] = features_ref[...]
        for h in range(2):
            left[1, :, h * HALF : (h + 1) * HALF] = panel[h, rows_at(row + 1, ND), :]
        for m, (dx, dy) in enumerate(plane):
            early_copy(m + 1, dx, dy).start()
        left_in[0] = left[:, :, rows_at(x, TILE)]

    own_part = jnp.dot(features_ref[...], self_v[...], preferred_element_type=F32)
    for load in loads[5:]:
        load.wait()
    degree = jnp.broadcast_to(degree_ref[...].astype(F32), (ND, ND))
    eye = lax.broadcasted_iota(jnp.int32, (ND, ND), 0) == lax.broadcasted_iota(jnp.int32, (ND, ND), 1)
    scale = lax.rsqrt(jnp.sum(jnp.where(eye, degree, 0.0), axis=1, keepdims=True))
    for copy in far:
        copy.wait_recv()
    for h in range(2):
        lanes = slice(h * HALF, (h + 1) * HALF)
        own_sums[:, lanes] = total(own_sums[:, lanes], [in_c[h, k] for k in (1, 2, 3)])
    sums = own_sums[...]

    aggregated = (sums * scale).astype(BF16)
    ours[...] = aggregated

    def left_copy(m, dx, dy, source_core):
        to = (z_lo * 2 + 1, lax.div(col, 16) * 16 + flip(x, dx, 2) * 4 + flip(y, dy, 2))
        return pltpu.make_async_remote_copy(
            src_ref=ours.at[:, rows_at(flip(x, dx, 2), TILE)], dst_ref=left_in.at[m, source_core],
            send_sem=l_s.at[m, source_core], recv_sem=l_r.at[m, source_core], device_id=to, device_id_type=MESH,
        )

    square = [(0, 0)] + plane
    for m, (dx, dy) in enumerate(square):
        if m:
            left_copy(m, dx, dy, core).start()

    @pl.when(core == 0)
    def _():
        left_copy(0, 0, 0, 0).start()

    @pl.when(core == 1)
    def _():
        left_in[0, 1] = ours[:, rows_at(x, TILE)]

    before = own_part + jnp.dot(aggregated, neigh_v[...], preferred_element_type=F32)
    sigma = 1.0 / (1.0 + jnp.exp(-before))
    gate = (cotangent_ref[...].astype(F32) * sigma * (1.0 + before * (1.0 - sigma))).astype(BF16)
    hidden_ref[...] = (before * sigma).astype(BF16)
    gated[...] = gate
    swaps = []
    for m, (dx, dy) in enumerate(square):
        lanes = rows_at(flip(y, dy, 2), TILE)
        for dc in range(2):
            if m or dc:
                swaps.append(
                    send(
                        gated.at[:, lanes], gated_in.at[m, core], g_s.at[m, dc], g_r.at[m, dc],
                        peer(dx=dx, dy=dy, dc=dc),
                    )
                )
    gated_in[0, core] = gated[:, rows_at(y, TILE)]

    @pl.when(core == 0)
    def _():
        for m, (dx, dy) in enumerate(plane):
            early_copy(m + 1, dx, dy).wait_recv()

    @pl.when(core == 1)
    def _():
        left_copy(0, 0, 0, 0).wait_recv()
        for m, (dx, dy) in enumerate(square):
            if m:
                left_copy(m, dx, dy, 0).wait_recv()
                left_copy(m, dx, dy, 1).wait_recv()

    for copy in swaps:
        copy.wait_recv()
    section[...] = lax.dot_general(
        left_in[...].reshape(16 * 2 * ND, TILE),
        gated_in[...].reshape(16 * 2 * ND, TILE),
        (((0,), (0,)), ((), ())),
        preferred_element_type=F32,
    ).reshape(4, ND, TILE)

    near = [
        send(section.at[flip(z_in, m, 2)], in_z.at[m], z_s.at[m], z_r.at[m], peer(dz=m)) for m in (2, 1, 3)
    ]
    for copy in near:
        copy.wait_recv()
    groups[z_group] = (section[z_in] + in_z[1] + in_z[2] + in_z[3]).astype(BF16)
    pl.semaphore_wait(word.at[1], 1)
    spread = [
        send(groups.at[z_group], groups.at[z_group], zs_s.at[m], zs_r.at[m], peer(dz=4 * m))
        for m in (4, 3, 5, 2, 6, 1, 7)
    ]
    for copy in spread:
        copy.wait_recv()
    final[0] = total(groups[0], [groups[k] for k in range(1, 8)]).astype(BF16)
    back = [send(final.at[0], final.at[m], za_s.at[m], za_r.at[m], peer(dz=m)) for m in (2, 1, 3)]

    to_plane = [peer(dx=dx, dy=dy) for dx, dy in plane]
    pieces = (slice(0, 1), slice(1, 2), slice(2, 4))
    out = []
    for k, piece in enumerate(pieces):
        for copy in ((), back[1:2], back[::2])[k]:
            copy.wait_recv()
        mine_there = parts.at[core, x, y, piece]
        out.append(
            [
                send(final.at[piece], mine_there, xy_s.at[k, m], xy_r.at[k, m], to)
                for m, to in enumerate(to_plane)
            ]
        )
    last = [[], []]

    def put(c, xb, yb, lo, value):
        for m in range(2):
            grads_ref[rows_at(c * 16 + xb * 4 + flip(z_in, lo + m, 2), ND), rows_at(yb, TILE)] = value[m]

    for part in range(2):
        both = slice(part * 2, part * 2 + 2)
        theirs = parts.at[core, x, y, both]
        last[part].append(send(final.at[both], theirs, xc_s.at[part, 0], xc_r.at[part, 0], partner))
        put(core, x, y, part * 2, final[both])
        for m, (dx, dy) in enumerate(plane):
            for copies in (out[:2], out[2:])[part]:
                copies[m].wait_recv()
            xb, yb = flip(x, dx, 2), flip(y, dy, 2)
            theirs = parts.at[core, xb, yb, both]
            last[part].append(send(theirs, theirs, xc_s.at[part, m + 1], xc_r.at[part, m + 1], partner))
            put(core, xb, yb, part * 2, parts[core, xb, yb, both])
    for part in range(2):
        for (dx, dy), copy in zip(square, last[part]):
            copy.wait_recv()
            xb, yb = flip(x, dx, 2), flip(y, dy, 2)
            put(1 - core, xb, yb, part * 2, parts[1 - core, xb, yb, part * 2 : part * 2 + 2])
    for m, (dx, dy) in enumerate(square):
        if m:
            left_copy(m, dx, dy, core).wait_send()

    @pl.when(core == 0)
    def _():
        left_copy(0, 0, 0, 0).wait_send()
        for m, (dx, dy) in enumerate(plane):
            early_copy(m + 1, dx, dy).wait_send()

    for copy in sent:
        copy.wait_send()


def per_device(features, self_weight, neigh_weight, tiles, tile_pos, tile_count, degree, cotangent):
    capacity = tiles.shape[1]
    vmem, hbm = pl.BlockSpec(memory_space=pltpu.VMEM), pl.BlockSpec(memory_space=pltpu.HBM)
    dma = pltpu.SemaphoreType.DMA
    hidden, grads = pl.pallas_call(
        kernel,
        out_shape=(
            jax.ShapeDtypeStruct((ND, WIDTH), BF16),
            jax.ShapeDtypeStruct((2 * WIDTH, WIDTH), BF16),
        ),
        in_specs=[hbm] * 8,
        out_specs=(vmem, vmem),
        scratch_shapes=[
            pltpu.VMEM((ND, WIDTH), BF16),
            pltpu.VMEM((1, 32), jnp.int32),
            pltpu.SMEM((1, 1), jnp.int32),
            pltpu.VMEM((64, TILE), jnp.int32),
            pltpu.SMEM((64, TILE), jnp.int32),
            pltpu.VMEM((1, ND), jnp.int32),
            pltpu.VMEM((ND, WIDTH), BF16),
            pltpu.VMEM((capacity, TILE, TILE), BF16),
            pltpu.VMEM((WIDTH, WIDTH), BF16),
            pltpu.VMEM((WIDTH, WIDTH), BF16),
            pltpu.VMEM((16, TILE, WIDTH), BF16),
            pltpu.VMEM((2, WIDTH, HALF), BF16),
            pltpu.VMEM((2, 4, 4, TILE, TILE), BF16),
            pltpu.VMEM((2, 4, 4, TILE, TILE), BF16),
            pltpu.VMEM((2, 4, TILE, TILE), F32),
            pltpu.VMEM((2, 4, TILE, TILE), F32),
            pltpu.VMEM((2, 4, 4, TILE, TILE), BF16),
            pltpu.VMEM((2, 4, 4, TILE, TILE), BF16),
            pltpu.VMEM((2, 4, TILE, TILE), BF16),
            pltpu.VMEM((2, 4, TILE, TILE), BF16),
            pltpu.VMEM((2, 4, TILE, TILE), BF16),
            pltpu.VMEM((2, 4, TILE, TILE), BF16),
            pltpu.VMEM((2, 4, ND, HALF), BF16),
            pltpu.VMEM((ND, WIDTH), F32),
            pltpu.VMEM((2, 4, ND, HALF), BF16),
            pltpu.VMEM((ND, WIDTH), BF16),
            pltpu.VMEM((2, ND, WIDTH), BF16),
            pltpu.VMEM((ND, WIDTH), BF16),
            pltpu.VMEM((16, 2, ND, TILE), BF16),
            pltpu.VMEM((16, 2, ND, TILE), BF16),
            pltpu.VMEM((4, ND, TILE), F32),
            pltpu.VMEM((4, ND, TILE), F32),
            pltpu.VMEM((8, ND, TILE), BF16),
            pltpu.VMEM((4, ND, TILE), BF16),
            pltpu.VMEM((2, 4, 4, 4, ND, TILE), BF16),
            pltpu.SemaphoreType.REGULAR((2,)),
            dma((9,)),
            *[dma((2, 8))] * 8,
            *[dma((2, 4))] * 2,
            *[dma((16,))] * 2,
            *[dma((16, 2))] * 4,
            *[dma((4,))] * 2,
            *[dma((8,))] * 2,
            *[dma((4,))] * 2,
            *[dma((3, 16))] * 2,
            *[dma((2, 16))] * 2,
        ],
        compiler_params=pltpu.CompilerParams(
            collective_id=0, has_side_effects=True, vmem_limit_bytes=60 * 1024 * 1024
        ),
        name="sage_layer",
    )(features, self_weight, neigh_weight, tiles[0], tile_pos, tile_count, degree[None, :], cotangent)
    return (hidden, grads[:WIDTH].astype(F32), grads[WIDTH:].astype(F32))


def solution(mesh):
    in_specs = (
        P(("row", "col"), None),
        P(),
        P(),
        P("row", "col", None, None),
        P("row", "col"),
        P("row", "col"),
        P(("row", "col")),
        P(("row", "col"), None),
    )
    out_specs = (P(("row", "col"), None), P(), P())
    return jax.shard_map(
        per_device, mesh=mesh, in_specs=in_specs, out_specs=out_specs, check_vma=False
    )
```
